1024 devices in a mesh: row: 32 (over z), col: 32 (over x, y, core).
Axes of the slice: x: 4, y: 4, z: 32, core: 2. Of those that a mesh axis runs over, the one named last changes fastest.
Arguments:
- values: bfloat16 [128, 32, 128, 128], P('row', 'col'), may hold values from -0.1875 to 0.1875
- column_slot_index: int32 [128, 32], P('row', 'col'), may hold values from 0 to 3
- branches: int32 [2], replicated, may hold values from 0 to 1, as said below
Outputs:
- purified: bfloat16 [128, 32, 128, 128], P('row', 'col')
The draws below stay inside these ranges and needn't reach their ends.
Inputs may be any that keep to these rules, and one draw needn't show every extreme that they name: column_slot_index[i, c] places block row i's single nonzero block among the 4 block columns of col index c. Branch 0 squares, branch 1 takes 2 X - X X; consecutive steps take different branches.
All inputs are finite; a program needn't handle non-finite values.
Results may differ from the reference program's by a relative error of at most 0.0051.
Values may be sent and summed in bfloat16 or wider, within the bound.
No kernel may reach another device: no remote copies, remote signals or barrier semaphores. Data moves between devices by JAX's collectives and lax.ppermute only.
A program may use at most 32 MiB of HBM per device.

```python
import jax
import jax.numpy as jnp
from jax import lax

BS = 128
BPD = 4
STEPS = 2
NBR = 128
N_COL = 32


def draw_branches(key, part):
    key = jax.random.fold_in(key, 7)
    first = jax.random.randint(key, (1,), 0, 2, dtype=jnp.int32)
    return ((first + jnp.arange(STEPS, dtype=jnp.int32)) % 2).astype(jnp.int32)


def plant(drawn, key, low, top_value):
    longest = drawn.shape.index(max(drawn.shape))
    spots = []
    for shift in (0, 1):
        where = [jax.random.randint(jax.random.fold_in(key, axis), (), 0, length) for axis, length in enumerate(drawn.shape)]
        where[longest] = (where[longest] + shift) % drawn.shape[longest]
        spots.append(tuple(where))
    return drawn.at[spots[0]].set(low).at[spots[1]].set(top_value)


def block_scale(key, dims, cuts, smallest, high):
    level, own = 1.0, jax.random.fold_in(key, 6)
    for position, parts in cuts:
        draws = jnp.exp(jax.random.uniform(jax.random.fold_in(own, position), (parts,), jnp.float32, smallest / len(cuts), high / len(cuts)))
        level = level * jnp.repeat(draws, dims[position] // parts).reshape([-1 if axis == position else 1 for axis in range(len(dims))])
    return level


def normal_values(rng, extent, deviation, reach, cuts=(), kind=jnp.bfloat16):
    level = block_scale(rng, extent, cuts, -0.22, 0.18) if cuts else 1.0
    entries = jax.random.normal(rng, extent, jnp.float32) * deviation * level
    return jnp.minimum(jnp.maximum(entries, -reach), reach).astype(kind)


def setup_inputs(seed: int = 0) -> dict:
    key_of = jax.random.split(jax.random.key(seed), 4)
    values = normal_values(key_of[0], (NBR, N_COL, BS, BS), (BS * N_COL // BPD) ** -0.5, 0.1875, ((0, 32), (1, 32)))
    column_slot_index = plant(jax.random.randint(key_of[1], (NBR, N_COL), 0, BPD), jax.random.fold_in(key_of[1], 1), 0, BPD - 1).astype(jnp.int32)
    branches = draw_branches(jax.random.fold_in(key_of[3], 71), 0)
    return {"values": values, "column_slot_index": column_slot_index, "branches": branches}


def reference(values, column_slot_index, branches):
    state = values
    for step in range(STEPS):
        def single_block_row(pair):
            row_vals, row_ids = pair
            desired_trace = jnp.arange(N_COL, dtype=jnp.int32) * BPD + row_ids.astype(jnp.int32)
            selected_blocks = state[desired_trace].astype(jnp.float32)
            match = column_slot_index[desired_trace] == row_ids[None, :]
            selected_blocks = jnp.where(match[:, :, None, None], selected_blocks, jnp.zeros_like(selected_blocks))
            return jnp.einsum('pab,pqbd->qad', row_vals.astype(jnp.float32), selected_blocks)
        matrix_square = lax.map(single_block_row, (state, column_slot_index))
        twice_density = 2.0 * state.astype(jnp.float32) - matrix_square
        newer = jnp.where(branches[step] == 1, twice_density, matrix_square)
        state = newer.astype(jnp.bfloat16)
    return state
```

```python
import functools

import jax
import jax.numpy as jnp
from jax import lax
from jax.experimental import pallas as pl
from jax.experimental.pallas import tpu as pltpu
from jax.sharding import Mesh, PartitionSpec as P

BPD = 4
STEPS = 2
BS = 128
ROWS = 4 * BS
AXES = ("zh", "zl", "x", "y", "core")
SIZES = (8, 4, 4, 4, 2)
BATCHES = ((0, 1, 7, 2, 6), (3, 5, 4))
RING = (0, 1, 3, 2)


def shift(size, by):
    return [(i, (i + by) % size) for i in range(size)]


def swap_pairs():
    pairs = []
    for zh in range(8):
        for zl in range(4):
            for x in range(4):
                for w in range(8):
                    pairs.append((((zh * 4 + zl) * 4 + x) * 8 + w, ((zh * 4 + x) * 4 + zl) * 8 + w))
    return pairs


def ring4(part, axis):
    one = lax.ppermute(part, axis, shift(4, 1))
    three = lax.ppermute(part, axis, shift(4, -1))
    half = part.shape[0] // 32 * 16
    two_a = lax.ppermute(one[:half], axis, shift(4, 1))
    two_b = lax.ppermute(three[half:], axis, shift(4, -1))
    return [part, one, three, two_a, two_b]


def kernel(rows, a_sizes, b_sizes, branch, tab, sa, sb, own, *refs):
    a_parts, refs = refs[: len(a_sizes)], refs[len(a_sizes) :]
    b_parts, refs = refs[: len(b_sizes)], refs[len(b_sizes) :]
    out, a_all, b_all, acc, sems = refs
    copies = []
    for parts, sizes, whole in ((a_parts, a_sizes, a_all), (b_parts, b_sizes, b_all)):
        at = 0
        for part, size in zip(parts, sizes):
            copies.append(
                pltpu.make_async_copy(part, whole.at[pl.ds(at, size)], sems.at[len(copies)])
            )
            at += size
    for copy in copies:
        copy.start()
    acc[...] = jnp.zeros_like(acc)
    mine = [sa[tab[64] * 4 + j] for j in range(4)]
    for copy in copies:
        copy.wait()

    def step(p, carry):
        la, lb = tab[p], tab[32 + p]
        for j in range(4):
            m = sa[la * 4 + j]

            @pl.when(sb[lb * 4 + m] == mine[j])
            def _():
                left = a_all[pl.ds(pl.multiple_of(la * rows + j * BS, 16), BS), :]
                right = b_all[pl.ds(pl.multiple_of(lb * rows + m * BS, 16), BS), :]
                acc[j * BS : (j + 1) * BS, :] += jnp.dot(
                    left, right, preferred_element_type=jnp.float32
                )

        return carry

    lax.fori_loop(0, 32, step, 0)
    square = acc[...]
    twice = 2.0 * own[...].astype(jnp.float32) - square
    out[...] = jnp.where(branch[0] == 1, twice, square).astype(out.dtype)


def multiply(branch, tab, sa, sb, own, a_parts, b_parts, rows):
    a_sizes = [q.shape[0] for q in a_parts]
    b_sizes = [q.shape[0] for q in b_parts]
    smem = pl.BlockSpec(memory_space=pltpu.SMEM)
    vmem = pl.BlockSpec(memory_space=pltpu.VMEM)
    anywhere = pl.BlockSpec(memory_space=pl.ANY)
    return pl.pallas_call(
        functools.partial(kernel, rows, a_sizes, b_sizes),
        out_shape=jax.ShapeDtypeStruct((ROWS, BS), jnp.bfloat16),
        in_specs=[smem] * 4 + [vmem] + [anywhere] * (len(a_parts) + len(b_parts)),
        out_specs=vmem,
        scratch_shapes=[
            pltpu.VMEM((32 * rows, BS), jnp.bfloat16),
            pltpu.VMEM((32 * rows, BS), jnp.bfloat16),
            pltpu.VMEM((ROWS, BS), jnp.float32),
            pltpu.SemaphoreType.DMA((len(a_parts) + len(b_parts),)),
        ],
        compiler_params=pltpu.CompilerParams(vmem_limit_bytes=24 * 1024 * 1024),
        cost_estimate=pl.CostEstimate(
            flops=2 * 128 * BS**3, bytes_accessed=64 * ROWS * BS * 2, transcendentals=0
        ),
    )(branch, tab, sa, sb, own, *a_parts, *b_parts)


def slots_of(parts, rows):
    found, at = [], 0
    for part in parts:
        size = part.shape[0]
        first = -(-(at - ROWS) // rows)
        for unit in range(max(first, 0), 32):
            row = unit * rows + ROWS - at
            if row >= size:
                break
            if row >= 0:
                found.append(part[row, :4])
        at += size
    return jnp.concatenate(found).astype(jnp.int32)


def places(zh, zl, x, y, core):
    p = jnp.arange(32, dtype=jnp.int32)
    ring = jnp.array([0, 1, 3, 2], jnp.int32)

    def pick(table, index):
        out = jnp.zeros_like(index)
        for k, value in enumerate(table):
            out = jnp.where(index == k, value, out)
        return out

    del ring
    order = [RING.index(k) for k in range(4)]
    la = ((p % 2) ^ core) * 16 + pick(order, (y - p // 2 % 4) % 4) * 4 + p // 8
    dz, dx = (zh - p // 4) % 8, pick(order, (x - p % 4) % 4)
    first, second = BATCHES
    at_first = pick([first.index(k) if k in first else 0 for k in range(8)], dz)
    at_second = pick([second.index(k) if k in second else 0 for k in range(8)], dz)
    is_first = pick([int(k in first) for k in range(8)], dz)
    n1, n2 = len(first), len(second)
    lb = jnp.where(is_first == 1, dx * n1 + at_first, 4 * n1 + dx * n2 + at_second)
    return jnp.concatenate([la, lb, jnp.full((1,), zl, jnp.int32)])


def gather(unit):
    at = {0: unit}
    for hop in (1, 2, 3):
        at[hop] = lax.ppermute(at[hop - 1], "zh", shift(8, 1))
        at[8 - hop] = lax.ppermute(at[(9 - hop) % 8], "zh", shift(8, -1))
    at[4] = lax.ppermute(at[3], "zh", shift(8, 1))
    near = lax.all_gather(unit, "zl", axis=0, tiled=True)
    half = ring4(near, "y")
    half = jnp.concatenate(half)
    other = lax.ppermute(half, "core", shift(2, 1))
    b_parts = []
    for batch in BATCHES:
        b_parts += ring4(jnp.concatenate([at[k] for k in batch]), "x")
    return [half, other], b_parts


def body(values, column_slot_index, branches):
    where = [lax.axis_index(name) for name in AXES]
    tab = places(*where)
    flat = values.reshape(ROWS, BS)
    tail = jnp.pad(column_slot_index[:, 0].astype(jnp.bfloat16)[None], ((0, 15), (0, BS - 4)))
    unit = lax.ppermute(jnp.concatenate([flat, tail]), AXES, swap_pairs())
    sa = sb = None
    for step in range(STEPS):
        rows = unit.shape[0]
        a_parts, b_parts = gather(unit)
        if step == 0:
            sa, sb = slots_of(a_parts, rows), slots_of(b_parts, rows)
        own = unit[:ROWS]
        unit = multiply(branches[step : step + 1], tab, sa, sb, own, a_parts, b_parts, rows)
    out = lax.ppermute(unit, AXES, swap_pairs())
    return out.reshape(values.shape)


def solution(mesh):
    fine = Mesh(mesh.devices.reshape(SIZES), AXES)
    split = (("zh", "zl"), ("x", "y", "core"))
    in_specs = (P(*split, None, None), P(*split), P())
    return jax.shard_map(
        body, mesh=fine, in_specs=in_specs, out_specs=P(*split, None, None), check_vma=False
    )
```

```python
import functools

import jax
import jax.numpy as jnp
import numpy as np
from jax import lax
from jax.experimental import pallas as pl
from jax.experimental.pallas import tpu as pltpu
from jax.sharding import Mesh, PartitionSpec as P

STEPS = 2
BS = 128
ROWS = 4 * BS
TAIL = 16
AXES = ("zh", "zl", "x", "y", "core")
SIZES = (8, 4, 4, 4, 2)
BATCHES = ((0, 1, 7, 2, 6), (3, 5), (4,))


def shift(size, by):
    return [(i, (i + by) % size) for i in range(size)]


def swap_pairs(by=0):
    pairs = []
    for i in range(1024):
        zh, zl, x, y, core = np.unravel_index(i, SIZES)
        pairs.append((i, int(np.ravel_multi_index(((zh + by) % 8, x, zl, y, core), SIZES))))
    return pairs


def ring4(batch, rows):
    offsets, units = batch
    part = jnp.concatenate(units) if len(units) > 1 else units[0]
    one = lax.ppermute(part, "x", shift(4, 1))
    three = lax.ppermute(part, "x", shift(4, -1))
    placed = [(part, 0, offsets), (one, 1, offsets), (three, 3, offsets)]
    if len(units) == 1:
        placed.append((lax.ppermute(part, "x", shift(4, 2)), 2, offsets))
    else:
        cut = len(units) // 2
        placed.append((lax.ppermute(one[: cut * rows], "x", shift(4, 1)), 2, offsets[:cut]))
        placed.append((lax.ppermute(three[cut * rows :], "x", shift(4, -1)), 2, offsets[cut:]))
    return placed


def kernel(rows, units, first, branch, tab, *refs):
    slots_in, refs = (None, refs) if first else (refs[0], refs[1:])
    own, a_all, refs = refs[0], refs[1], refs[2:]
    parts, refs = refs[: len(units)], refs[len(units) :]
    if first:
        out, slots_out, acc, slots, sem = refs
        for k in range(32):
            row = a_all[k * rows + ROWS : (k + 1) * rows, :].astype(jnp.float32)[0:1]
            slots_out[k : k + 1, :] = row.astype(jnp.int32)
        at = 32
        for part, n in zip(parts, units):
            for k in range(n):
                row = part[k * rows + ROWS : (k + 1) * rows, :].astype(jnp.float32)[0:1]
                slots_out[at : at + 1, :] = row.astype(jnp.int32)
                at += 1
        copy = pltpu.make_async_copy(slots_out, slots, sem)
        copy.start()
        acc[...] = jnp.zeros_like(acc)
        copy.wait()
    else:
        out, acc = refs
        slots = slots_in
        acc[...] = jnp.zeros_like(acc)
    mine = [slots[tab[32], j] for j in range(4)]

    def unit(part, start, k, carry):
        la = tab[start + k]
        for j in range(4):
            m = slots[la, j]

            @pl.when(slots[32 + start + k, m] == mine[j])
            def _():
                left = a_all[pl.ds(pl.multiple_of(la * rows + j * BS, 16), BS), :]
                right = part[pl.ds(pl.multiple_of(k * rows + m * BS, 16), BS), :]
                acc[j * BS : (j + 1) * BS, :] += jnp.dot(
                    left, right, preferred_element_type=jnp.float32
                )

        return carry

    at = 0
    for part, n in zip(parts, units):
        if n == 1:
            unit(part, at, 0, 0)
        else:
            lax.fori_loop(0, n, functools.partial(unit, part, at), 0)
        at += n
    square = acc[...]
    twice = 2.0 * own[:ROWS, :].astype(jnp.float32) - square
    out[...] = jnp.where(branch[0] == 1, twice, square).astype(out.dtype)


def multiply(branch, tab, slots, own, a_all, parts):
    first, rows = slots is None, own.shape[0]
    units = [part.shape[0] // rows for part in parts]
    smem = pl.BlockSpec(memory_space=pltpu.SMEM)
    vmem = pl.BlockSpec(memory_space=pltpu.VMEM)
    out_shape = [jax.ShapeDtypeStruct((ROWS, BS), jnp.bfloat16)]
    scratch = [pltpu.VMEM((ROWS, BS), jnp.float32)]
    if first:
        out_shape.append(jax.ShapeDtypeStruct((64, BS), jnp.int32))
        scratch += [pltpu.SMEM((64, BS), jnp.int32), pltpu.SemaphoreType.DMA]
    done = pl.pallas_call(
        functools.partial(kernel, rows, units, first),
        out_shape=out_shape,
        in_specs=[smem] * (2 if first else 3) + [vmem] * (2 + len(parts)),
        out_specs=[vmem] * len(out_shape),
        scratch_shapes=scratch,
        compiler_params=pltpu.CompilerParams(vmem_limit_bytes=24 * 1024 * 1024),
        cost_estimate=pl.CostEstimate(
            flops=2 * 128 * BS**3, bytes_accessed=64 * ROWS * BS * 2, transcendentals=0
        ),
    )(branch, tab, *([] if first else [slots]), own, a_all, *parts)
    return done[0], done[1] if first else slots


def gather(unit, up, down):
    near = lax.all_gather(unit, "zl", axis=0, tiled=True)
    a_all = lax.all_gather(near, ("y", "core"), axis=0, tiled=True)
    at = {0: unit, 1: up, 7: down}
    for hop in (2, 3):
        at[hop] = lax.ppermute(at[hop - 1], "zh", shift(8, 1))
        at[8 - hop] = lax.ppermute(at[9 - hop], "zh", shift(8, -1))
    at[4] = lax.ppermute(at[3], "zh", shift(8, 1))
    placed = []
    for offsets in BATCHES:
        placed += ring4((offsets, [at[k] for k in offsets]), unit.shape[0])
    return a_all, placed


def table(placed):
    zh, zl, x, y, core = (lax.axis_index(name) for name in AXES)
    dz = np.concatenate([np.array(offsets) for _, _, offsets in placed])
    dx = np.concatenate([np.full(len(offsets), d) for _, d, offsets in placed])
    p = (zh - dz) % 8 * 4 + (x - dx) % 4
    la = p % 8 * 4 + p // 8
    return jnp.concatenate([la, jnp.reshape((y * 2 + core) * 4 + zl, (1,))]).astype(jnp.int32)


def body(values, column_slot_index, branches):
    flat = values.reshape(ROWS, BS)
    tail = column_slot_index[:, 0].astype(jnp.bfloat16)[None]
    start = jnp.concatenate([flat, jnp.pad(tail, ((0, TAIL - 1), (0, BS - 4)))])
    unit, up, down = (lax.ppermute(start, AXES, swap_pairs(by)) for by in (0, 1, -1))
    slots = None
    for step in range(STEPS):
        if step:
            up, down = (lax.ppermute(unit, "zh", shift(8, by)) for by in (1, -1))
        a_all, placed = gather(unit, up, down)
        unit, slots = multiply(
            branches[step : step + 1], table(placed), slots, unit, a_all, [q for q, _, _ in placed]
        )
    return lax.ppermute(unit, AXES, swap_pairs()).reshape(values.shape)


def solution(mesh):
    fine = Mesh(mesh.devices.reshape(SIZES), AXES)
    split = (("zh", "zl"), ("x", "y", "core"))
    in_specs = (P(*split, None, None), P(*split), P())
    return jax.shard_map(
        body, mesh=fine, in_specs=in_specs, out_specs=P(*split, None, None), check_vma=False
    )
```

```python
import functools

import jax
import jax.numpy as jnp
import numpy as np
from jax import lax
from jax.experimental import pallas as pl
from jax.experimental.pallas import tpu as pltpu
from jax.sharding import Mesh, PartitionSpec as P

STEPS = 2
BS = 128
ROWS = 4 * BS
TAIL = 16
AXES = ("zh", "zl", "x1", "x0", "y", "core")
SIZES = (8, 4, 2, 2, 4, 2)


def swap(zh, zl, x1, x0, y, core):
    return zh, x0 * 2 + core, x1, zl // 2, y, zl % 2


def hop(zh, zl, x1, x0, y, core):
    return (zh + 1 - 2 * core) % 8, zl, x1, x0, y, core


def flip(zh, zl, x1, x0, y, core):
    return zh, zl, x1, x0, y, 1 - core


def move(part, *steps):
    pairs = []
    for i in range(1024):
        place = tuple(int(k) for k in np.unravel_index(i, SIZES))
        for step in steps:
            place = step(*place)
        pairs.append((i, int(np.ravel_multi_index(place, SIZES))))
    return lax.ppermute(part, AXES, pairs)


def exchange(part, axis):
    return lax.ppermute(part, axis, [(0, 1), (1, 0)])


def kernel(rows, units, first, branch, tab, *refs):
    slots, refs = (None, refs) if first else (refs[0], refs[1:])
    own, a_hbm, refs = refs[0], refs[1], refs[2:]
    parts, refs = refs[: len(units)], refs[len(units) :]
    if first:
        out, slots_out, a_all, b_all, acc, sems, slots, sem = refs
    else:
        out, a_all, b_all, acc, sems = refs
    copies = [pltpu.make_async_copy(a_hbm, a_all, sems.at[0])]
    at = 0
    for part, n in zip(parts, units):
        copies.append(
            pltpu.make_async_copy(
                part, b_all.at[pl.ds(at * rows, n * rows)], sems.at[len(copies)]
            )
        )
        at += n
    for copy in copies:
        copy.start()
    nothing = 32 * rows
    b_all[nothing : nothing + BS, :] = jnp.zeros((BS, BS), jnp.bfloat16)
    acc[...] = jnp.zeros_like(acc)
    for copy in copies:
        copy.wait()
    if first:
        for base, whole in ((0, a_all), (32, b_all)):
            for k in range(32):
                row = whole[k * rows + ROWS : (k + 1) * rows, :].astype(jnp.float32)[0:1]
                slots_out[base + k : base + k + 1, :] = row.astype(jnp.int32)
        copy = pltpu.make_async_copy(slots_out, slots, sem)
        copy.start()
        copy.wait()
    mine = [slots[tab[32], j] for j in range(4)]

    def pair(t, carry):
        las = [tab[2 * t + k] for k in range(2)]
        for j in range(4):
            lefts, rights = [], []
            for k in range(2):
                m = slots[las[k], j]
                hit = slots[32 + 2 * t + k, m] == mine[j]
                right = jnp.where(hit, (2 * t + k) * rows + m * BS, nothing)
                rights.append(b_all[pl.ds(pl.multiple_of(right, 16), BS), :])
                left = las[k] * rows + j * BS
                lefts.append(a_all[pl.ds(pl.multiple_of(left, 16), BS), :])
            acc[j * BS : (j + 1) * BS, :] += jnp.dot(
                jnp.concatenate(lefts, 1),
                jnp.concatenate(rights, 0),
                preferred_element_type=jnp.float32,
            )
        return carry

    lax.fori_loop(0, 16, pair, 0)
    square = acc[...]
    twice = 2.0 * own[:ROWS, :].astype(jnp.float32) - square
    out[...] = jnp.where(branch[0] == 1, twice, square).astype(out.dtype)


def multiply(branch, tab, slots, own, a_all, parts):
    first, rows = slots is None, own.shape[0]
    units = [part.shape[0] // rows for part in parts]
    smem = pl.BlockSpec(memory_space=pltpu.SMEM)
    vmem = pl.BlockSpec(memory_space=pltpu.VMEM)
    anywhere = pl.BlockSpec(memory_space=pl.ANY)
    out_shape = [jax.ShapeDtypeStruct((ROWS, BS), jnp.bfloat16)]
    scratch = [
        pltpu.VMEM((32 * rows, BS), jnp.bfloat16),
        pltpu.VMEM((32 * rows + BS, BS), jnp.bfloat16),
        pltpu.VMEM((ROWS, BS), jnp.float32),
        pltpu.SemaphoreType.DMA((1 + len(parts),)),
    ]
    if first:
        out_shape.append(jax.ShapeDtypeStruct((64, BS), jnp.int32))
        scratch += [pltpu.SMEM((64, BS), jnp.int32), pltpu.SemaphoreType.DMA]
    done = pl.pallas_call(
        functools.partial(kernel, rows, units, first),
        out_shape=out_shape,
        in_specs=[smem] * (2 if first else 3) + [vmem] + [anywhere] * (1 + len(parts)),
        out_specs=[vmem] * len(out_shape),
        scratch_shapes=scratch,
        compiler_params=pltpu.CompilerParams(vmem_limit_bytes=16 * 1024 * 1024),
        cost_estimate=pl.CostEstimate(
            flops=2 * 128 * BS**3, bytes_accessed=64 * ROWS * BS * 2, transcendentals=0
        ),
    )(branch, tab, *([] if first else [slots]), own, a_all, *parts)
    return done[0], done[1] if first else slots


def gather(unit, sibling, hop1):
    rows = unit.shape[0]
    near = [unit]
    for by in (1, 2, 3):
        near.append(lax.ppermute(unit, "zl", [(i, (i + by) % 4) for i in range(4)]))
    a_all = lax.all_gather(jnp.concatenate(near), ("x1", "y"), axis=0, tiled=True)
    both = jnp.concatenate([unit, sibling])
    hops = [hop1]
    for _ in range(2):
        hops.append(move(hops[-1], hop))
    hops.append(move(hops[-1][:rows], hop))
    placed = [
        (both, [(0, 0, 0), (0, 0, 1)]),
        (exchange(both, "x0"), [(0, 1, 0), (0, 1, 1)]),
    ]
    for k, got in enumerate(hops, 1):
        line = jnp.concatenate([got, exchange(got, "x0")])
        names = [(k, f, w) for f in (0, 1) for w in range(2 if k < 4 else 1)]
        placed.append((line, names))
        placed.append((exchange(line, "core"), [(-h, f, 1 - w) for h, f, w in names]))
    return a_all, placed


def table(placed):
    zh, zl, x1, x0, y, core = (lax.axis_index(name) for name in AXES)
    names = np.concatenate([np.array(n) for _, n in placed])
    up = (1 - 2 * core) * names[:, 0]
    p = (zh - up) % 8 * 4 + (x0 ^ names[:, 1]) * 2 + (core ^ names[:, 2])
    low = p // 8 % 2 * 2 + p % 2
    la = (p // 16 * 4 + p // 2 % 4) * 4 + (zl - low) % 4
    return jnp.concatenate([la, jnp.reshape((x1 * 4 + y) * 4, (1,))]).astype(jnp.int32)


def body(values, column_slot_index, branches):
    flat = values.reshape(ROWS, BS)
    tail = column_slot_index[:, 0].astype(jnp.bfloat16)[None]
    start = jnp.concatenate([flat, jnp.pad(tail, ((0, TAIL - 1), (0, BS - 4)))])
    unit, sibling = move(start, swap), move(start, swap, flip)
    hop1 = jnp.concatenate([move(start, swap, hop), move(start, swap, flip, hop)])
    slots = None
    for step in range(STEPS):
        if step:
            sibling = exchange(unit, "core")
            hop1 = move(jnp.concatenate([unit, sibling]), hop)
        a_all, placed = gather(unit, sibling, hop1)
        unit, slots = multiply(
            branches[step : step + 1], table(placed), slots, unit, a_all, [q for q, _ in placed]
        )
    return move(unit, swap).reshape(values.shape)


def solution(mesh):
    fine = Mesh(mesh.devices.reshape(SIZES), AXES)
    split = (("zh", "zl"), ("x1", "x0", "y", "core"))
    in_specs = (P(*split, None, None), P(*split), P())
    return jax.shard_map(
        body, mesh=fine, in_specs=in_specs, out_specs=P(*split, None, None), check_vma=False
    )
```

```python
import functools

import jax
import jax.numpy as jnp
import numpy as np
from jax import lax
from jax.experimental import pallas as pl
from jax.experimental.pallas import tpu as pltpu
from jax.sharding import Mesh, PartitionSpec as P

STEPS = 2
BS = 128
ROWS = 4 * BS
TAIL = 16
AXES = ("zh", "zl", "x", "y", "core")
SIZES = (8, 4, 4, 4, 2)


def swap(zh, zl, x, y, core):
    return zh, x, zl, y, core


def hop(zh, zl, x, y, core):
    return (zh + 1 - 2 * core) % 8, zl, x, y, core


def flip(zh, zl, x, y, core):
    return zh, zl, x, y, 1 - core


def move(part, *steps):
    pairs = []
    for i in range(1024):
        place = tuple(int(k) for k in np.unravel_index(i, SIZES))
        for step in steps:
            place = step(*place)
        pairs.append((i, int(np.ravel_multi_index(place, SIZES))))
    return lax.ppermute(part, AXES, pairs)


def across(part, axis, mask):
    size = SIZES[AXES.index(axis)]
    return lax.ppermute(part, axis, [(i, i ^ mask) for i in range(size)])


def kernel(rows, picks, first, branch, tab, *refs):
    slots, refs = (None, refs) if first else (refs[0], refs[1:])
    own, a_hbm, refs = refs[0], refs[1], refs[2:]
    parts, refs = refs[: len(picks)], refs[len(picks) :]
    if first:
        out, slots_out, a_all, b_all, acc, sems, slots, sem = refs
    else:
        out, a_all, b_all, acc, sems = refs
    copies = [pltpu.make_async_copy(a_hbm, a_all, sems.at[0])]
    for part, wanted in zip(parts, picks):
        for k in wanted:
            at = len(copies)
            copies.append(
                pltpu.make_async_copy(
                    part.at[pl.ds(k * rows, rows)],
                    b_all.at[pl.ds((at - 1) * rows, rows)],
                    sems.at[at],
                )
            )
    for copy in copies:
        copy.start()
    nothing = 32 * rows
    b_all[nothing : nothing + BS, :] = jnp.zeros((BS, BS), jnp.bfloat16)
    acc[...] = jnp.zeros_like(acc)
    for copy in copies:
        copy.wait()
    if first:
        for base, whole in ((0, a_all), (32, b_all)):
            for k in range(32):
                row = whole[k * rows + ROWS : (k + 1) * rows, :].astype(jnp.float32)[0:1]
                slots_out[base + k : base + k + 1, :] = row.astype(jnp.int32)
        copy = pltpu.make_async_copy(slots_out, slots, sem)
        copy.start()
        copy.wait()
    mine = [slots[tab[32], j] for j in range(4)]

    def pair(t, carry):
        las = [tab[2 * t + k] for k in range(2)]
        for j in range(4):
            lefts, rights = [], []
            for k in range(2):
                m = slots[las[k], j]
                hit = slots[32 + 2 * t + k, m] == mine[j]
                right = jnp.where(hit, (2 * t + k) * rows + m * BS, nothing)
                rights.append(b_all[pl.ds(pl.multiple_of(right, 16), BS), :])
                left = las[k] * rows + j * BS
                lefts.append(a_all[pl.ds(pl.multiple_of(left, 16), BS), :])
            acc[j * BS : (j + 1) * BS, :] += jnp.dot(
                jnp.concatenate(lefts, 1),
                jnp.concatenate(rights, 0),
                preferred_element_type=jnp.float32,
            )
        return carry

    lax.fori_loop(0, 16, pair, 0)
    square = acc[...]
    twice = 2.0 * own[:ROWS, :].astype(jnp.float32) - square
    out[...] = jnp.where(branch[0] == 1, twice, square).astype(out.dtype)


def multiply(branch, tab, slots, own, a_all, placed):
    first, rows = slots is None, own.shape[0]
    parts = [part for part, _ in placed]
    picks = [list(names) for _, names in placed]
    smem = pl.BlockSpec(memory_space=pltpu.SMEM)
    vmem = pl.BlockSpec(memory_space=pltpu.VMEM)
    anywhere = pl.BlockSpec(memory_space=pl.ANY)
    out_shape = [jax.ShapeDtypeStruct((ROWS, BS), jnp.bfloat16)]
    scratch = [
        pltpu.VMEM((32 * rows, BS), jnp.bfloat16),
        pltpu.VMEM((32 * rows + BS, BS), jnp.bfloat16),
        pltpu.VMEM((ROWS, BS), jnp.float32),
        pltpu.SemaphoreType.DMA((33,)),
    ]
    if first:
        out_shape.append(jax.ShapeDtypeStruct((64, BS), jnp.int32))
        scratch += [pltpu.SMEM((64, BS), jnp.int32), pltpu.SemaphoreType.DMA]
    done = pl.pallas_call(
        functools.partial(kernel, rows, picks, first),
        out_shape=out_shape,
        in_specs=[smem] * (2 if first else 3) + [vmem] + [anywhere] * (1 + len(parts)),
        out_specs=[vmem] * len(out_shape),
        scratch_shapes=scratch,
        compiler_params=pltpu.CompilerParams(vmem_limit_bytes=52 * 1024 * 1024),
        cost_estimate=pl.CostEstimate(
            flops=2 * 128 * BS**3, bytes_accessed=64 * ROWS * BS * 2, transcendentals=0
        ),
    )(branch, tab, *([] if first else [slots]), own, a_all, *parts)
    return done[0], done[1] if first else slots


def together(*parts):
    return lax.optimization_barrier(parts)


def gather(unit, up, down):
    rows = unit.shape[0]
    near = [unit]
    for by in (1, 2, 3):
        near.append(lax.ppermute(unit, "zl", [(i, (i + by) % 4) for i in range(4)]))
    near = jnp.concatenate(near)
    near, up, down = together(near, up, down)
    a_all = lax.all_gather(near, ("y", "core"), axis=0, tiled=True)
    hop1 = jnp.concatenate([up, down])
    hop2 = move(hop1, hop)
    one0, one1 = across(unit, "x", 1), across(hop1, "x", 1)
    hop2, one0, one1 = together(hop2, one0, one1)

    hop3 = move(hop2, hop)
    two0 = across(jnp.concatenate([unit, one0]), "x", 3)
    two1 = across(jnp.concatenate([hop1, one1]), "x", 3)
    one2 = across(hop2, "x", 1)
    hop3, two0, two1, one2 = together(hop3, two0, two1, one2)

    hop4 = move(hop3[:rows], hop)
    two2, one3 = across(jnp.concatenate([hop2, one2]), "x", 3), across(hop3, "x", 1)
    far1 = to_other(rows, hop1, one1, two1)
    hop4, two2, one3, far1 = together(hop4, two2, one3, far1)

    two3 = across(jnp.concatenate([hop3, one3]), "x", 3)
    last = [across(hop4, "x", f) for f in (1, 3, 2)]
    far2 = to_other(rows, hop2, one2, two2)
    two3, far2, *last = together(two3, far2, *last)

    far3 = to_other(rows, hop3, one3, two3)
    placed = [(unit, {0: (0, 0)}), (one0, {0: (0, 1)}), (two0, {0: (0, 3), 1: (0, 2)})]
    for k, one, two, three, far in ((1, hop1, one1, two1, far1), (2, hop2, one2, two2, far2)):
        placed += parted(k, one, two, three, far)
    placed += [(hop4, {0: (4, 0)})] + [(q, {0: (4, f)}) for q, f in zip(last, (1, 3, 2))]
    placed += parted(3, hop3, one3, two3, far3)
    return a_all, placed


def to_other(rows, got, one, two):
    theirs = [got[rows:], one[rows:], two[rows : 2 * rows], two[3 * rows :]]
    return across(jnp.concatenate(theirs), "core", 1)


def parted(k, got, one, two, far):
    return [
        (got, {0: (k, 0)}),
        (one, {0: (k, 1)}),
        (two, {0: (k, 3), 2: (k, 2)}),
        (far, {i: (-k, f) for i, f in enumerate((0, 1, 3, 2))}),
    ]


def table(placed):
    zh, zl, x, y, core = (lax.axis_index(name) for name in AXES)
    names = np.concatenate([np.array(list(n.values())) for _, n in placed])
    p = (zh - (1 - 2 * core) * names[:, 0]) % 8 * 4 + (x ^ names[:, 1])
    la = p % 8 * 4 + (zl - p // 8) % 4
    return jnp.concatenate([la, jnp.reshape((y * 2 + core) * 4, (1,))]).astype(jnp.int32)


def body(values, column_slot_index, branches):
    flat = values.reshape(ROWS, BS)
    tail = column_slot_index[:, 0].astype(jnp.bfloat16)[None]
    start = jnp.concatenate([flat, jnp.pad(tail, ((0, TAIL - 1), (0, BS - 4)))])
    unit, up, down = (move(start, swap, *more) for more in ((), (hop,), (flip, hop)))
    slots = None
    for step in range(STEPS):
        if step:
            up, down = move(unit, hop), move(unit, flip, hop)
        a_all, placed = gather(unit, up, down)
        unit, slots = multiply(
            branches[step : step + 1], table(placed), slots, unit, a_all, placed
        )
    return move(unit, swap).reshape(values.shape)


def solution(mesh):
    fine = Mesh(mesh.devices.reshape(SIZES), AXES)
    split = (("zh", "zl"), ("x", "y", "core"))
    in_specs = (P(*split, None, None), P(*split), P())
    return jax.shard_map(
        body, mesh=fine, in_specs=in_specs, out_specs=P(*split, None, None), check_vma=False
    )
```

```python
import functools

import jax
import jax.numpy as jnp
import numpy as np
from jax import lax
from jax.experimental import pallas as pl
from jax.experimental.pallas import tpu as pltpu
from jax.sharding import Mesh, PartitionSpec as P

STEPS = 2
BS = 128
ROWS = 4 * BS
LIST = 40
TAIL = 16
AXES = ("zh", "zl", "x", "y", "core")
SIZES = (16, 2, 4, 4, 2)


def swap(zh, zl, x, y, core):
    return zh, core, x, y, zl


def hop(zh, zl, x, y, core):
    return (zh + 1 - 2 * core) % 16, zl, x, y, core


def pair(zh, zl, x, y, core):
    return zh, 1 - zl, x, y, core


def flip(zh, zl, x, y, core):
    return zh, zl, x, y, 1 - core


def move(part, *steps):
    pairs = []
    for i in range(1024):
        place = tuple(int(k) for k in np.unravel_index(i, SIZES))
        for step in steps:
            place = step(*place)
        pairs.append((i, int(np.ravel_multi_index(place, SIZES))))
    return lax.ppermute(part, AXES, pairs)


def across(part, axis, mask):
    size = SIZES[AXES.index(axis)]
    return lax.ppermute(part, axis, [(i, i ^ mask) for i in range(size)])


def kernel(rows, units, first, branch, tab, *refs):
    slots, refs = (None, refs) if first else (refs[0], refs[1:])
    own, a_hbm, refs = refs[0], refs[1], refs[2:]
    parts, refs = refs[: len(units)], refs[len(units) :]
    if first:
        out, slots_out, a_all, b_all, lefts, rights, sems, slots, sem = refs
    else:
        out, a_all, b_all, lefts, rights, sems = refs
    copies = [pltpu.make_async_copy(a_hbm, a_all, sems.at[0])]
    at = 0
    for part, n in zip(parts, units):
        copies.append(
            pltpu.make_async_copy(
                part, b_all.at[pl.ds(at * rows, n * rows)], sems.at[len(copies)]
            )
        )
        at += n
    for copy in copies:
        copy.start()
    nothing = 32 * rows
    b_all[nothing : nothing + BS, :] = jnp.zeros((BS, BS), jnp.bfloat16)

    def listed():
        mine = [slots[tab[32], j] for j in range(4)]

        def scan(p, counts):
            la, more = tab[p], []
            for j in range(4):
                m = slots[la, j]
                lefts[j * LIST + counts[j]] = la * rows + j * BS
                rights[j * LIST + counts[j]] = p * rows + m * BS
                more.append(counts[j] + (slots[32 + p, m] == mine[j]).astype(jnp.int32))
            return tuple(more)

        counts = lax.fori_loop(0, 32, scan, (jnp.int32(0),) * 4)
        for j in range(4):
            for k in range(3):
                lefts[j * LIST + counts[j] + k] = 0
                rights[j * LIST + counts[j] + k] = nothing
        return counts

    if not first:
        counts = listed()
    for copy in copies:
        copy.wait()
    if first:
        for base, whole in ((0, a_all), (32, b_all)):
            for k in range(32):
                row = whole[k * rows + ROWS : (k + 1) * rows, :].astype(jnp.float32)[0:1]
                slots_out[base + k : base + k + 1, :] = row.astype(jnp.int32)
        copy = pltpu.make_async_copy(slots_out, slots, sem)
        copy.start()
        copy.wait()
        counts = listed()

    for j in range(4):

        def four(t, total):
            at = [j * LIST + 4 * t + k for k in range(4)]
            left = [a_all[pl.ds(pl.multiple_of(lefts[i], 16), BS), :] for i in at]
            right = [b_all[pl.ds(pl.multiple_of(rights[i], 16), BS), :] for i in at]
            return total + jnp.dot(
                jnp.concatenate(left, 1),
                jnp.concatenate(right, 0),
                preferred_element_type=jnp.float32,
            )

        square = lax.fori_loop(0, (counts[j] + 3) // 4, four, jnp.zeros((BS, BS), jnp.float32))
        block = pl.ds(j * BS, BS)
        twice = 2.0 * own[block, :].astype(jnp.float32) - square
        out[block, :] = jnp.where(branch[0] == 1, twice, square).astype(out.dtype)


def multiply(branch, tab, slots, own, a_all, placed):
    first, rows = slots is None, own.shape[0]
    parts = [part for part, _ in placed]
    units = [len(names) for _, names in placed]
    smem = pl.BlockSpec(memory_space=pltpu.SMEM)
    vmem = pl.BlockSpec(memory_space=pltpu.VMEM)
    anywhere = pl.BlockSpec(memory_space=pl.ANY)
    out_shape = [jax.ShapeDtypeStruct((ROWS, BS), jnp.bfloat16)]
    scratch = [
        pltpu.VMEM((32 * rows, BS), jnp.bfloat16),
        pltpu.VMEM((32 * rows + BS, BS), jnp.bfloat16),
        pltpu.SMEM((4 * LIST,), jnp.int32),
        pltpu.SMEM((4 * LIST,), jnp.int32),
        pltpu.SemaphoreType.DMA((1 + len(parts),)),
    ]
    if first:
        out_shape.append(jax.ShapeDtypeStruct((64, BS), jnp.int32))
        scratch += [pltpu.SMEM((64, BS), jnp.int32), pltpu.SemaphoreType.DMA]
    done = pl.pallas_call(
        functools.partial(kernel, rows, units, first),
        out_shape=out_shape,
        in_specs=[smem] * (2 if first else 3) + [vmem] + [anywhere] * (1 + len(parts)),
        out_specs=[vmem] * len(out_shape),
        scratch_shapes=scratch,
        compiler_params=pltpu.CompilerParams(vmem_limit_bytes=52 * 1024 * 1024),
        cost_estimate=pl.CostEstimate(
            flops=2 * 128 * BS**3, bytes_accessed=64 * ROWS * BS * 2, transcendentals=0
        ),
    )(branch, tab, *([] if first else [slots]), own, a_all, *parts)
    return done[0], done[1] if first else slots


def gather(unit, pal, sibling, up, down):
    rows = unit.shape[0]
    near = jnp.concatenate([unit, pal])
    near, sibling, up, down = lax.optimization_barrier((near, sibling, up, down))
    a_all = lax.all_gather(near, ("x", "y"), axis=0, tiled=True)
    chains, first, second = ring(up, down)
    last = move(chains[0][6], hop)
    final = across(jnp.concatenate([chains[0][6], chains[1][6], last]), "core", 1)
    placed = [(unit, {0: (0, 0)}), (sibling, {0: (0, 1)})]
    for k in range(7):
        placed += [(chain[k], {0: (k + 1, w)}) for w, chain in enumerate(chains)]
    for part, start in ((first, 1), (second, 4)):
        placed.append((part, {i: (-(i // 2 + start), 1 - i % 2) for i in range(6)}))
    placed += [(last, {0: (8, 0)}), (final, {0: (-7, 1), 1: (-7, 0), 2: (8, 1)})]
    return a_all, placed


def ring(up, down):
    chains = [[up], [down]]

    def on():
        for chain in chains:
            chain.append(move(chain[-1], hop))

    def to_other(a, b):
        return across(jnp.concatenate([chain[k] for k in range(a, b) for chain in chains]), "core", 1)

    for _ in range(4):
        on()
    first = to_other(0, 3)
    on()
    chains[0][5], chains[1][5], first = lax.optimization_barrier((chains[0][5], chains[1][5], first))
    on()
    second = to_other(3, 6)
    chains[0][6], chains[1][6], second = lax.optimization_barrier((chains[0][6], chains[1][6], second))
    return chains, first, second


def table(placed):
    zh, zl, x, y, core = (lax.axis_index(name) for name in AXES)
    names = np.concatenate([np.array(list(n.values())) for _, n in placed])
    p = (zh - (1 - 2 * core) * names[:, 0]) % 16 * 2 + (core ^ names[:, 1])
    la = p // 2 * 2 + (p % 2 ^ zl)
    return jnp.concatenate([la, jnp.reshape((x * 4 + y) * 2, (1,))]).astype(jnp.int32)


def body(values, column_slot_index, branches):
    flat = values.reshape(ROWS, BS)
    tail = column_slot_index[:, 0].astype(jnp.bfloat16)[None]
    start = jnp.concatenate([flat, jnp.pad(tail, ((0, TAIL - 1), (0, BS - 4)))])
    def firsts(part, *steps):
        return [move(part, *steps, *more) for more in ((pair,), (flip,), (hop,), (flip, hop))]

    unit, others = move(start, swap), firsts(start, swap)
    slots = None
    for step in range(STEPS):
        if step:
            others = firsts(unit)
        a_all, placed = gather(unit, *others)
        unit, slots = multiply(
            branches[step : step + 1], table(placed), slots, unit, a_all, placed
        )
    return move(unit, swap).reshape(values.shape)


def solution(mesh):
    fine = Mesh(mesh.devices.reshape(SIZES), AXES)
    split = (("zh", "zl"), ("x", "y", "core"))
    in_specs = (P(*split, None, None), P(*split), P())
    return jax.shard_map(
        body, mesh=fine, in_specs=in_specs, out_specs=P(*split, None, None), check_vma=False
    )
```

```python
import functools

import jax
import jax.numpy as jnp
import numpy as np
from jax import lax
from jax.experimental import pallas as pl
from jax.experimental.pallas import tpu as pltpu
from jax.sharding import Mesh, PartitionSpec as P

STEPS = 2
BS = 128
ROWS = 4 * BS
LIST = 40
TAIL = 16
AXES = ("zh", "zl", "x", "y", "core")
SIZES = (16, 2, 4, 4, 2)


def swap(zh, zl, x, y, core):
    return zh, core, x, y, zl


def hop(zh, zl, x, y, core):
    return (zh + 1 - 2 * core) % 16, zl, x, y, core


def pair(zh, zl, x, y, core):
    return zh, 1 - zl, x, y, core


def flip(zh, zl, x, y, core):
    return zh, zl, x, y, 1 - core


def move(part, *steps):
    pairs = []
    for i in range(1024):
        place = tuple(int(k) for k in np.unravel_index(i, SIZES))
        for step in steps:
            place = step(*place)
        pairs.append((i, int(np.ravel_multi_index(place, SIZES))))
    return lax.ppermute(part, AXES, pairs)


def across(part, axis, mask):
    size = SIZES[AXES.index(axis)]
    return lax.ppermute(part, axis, [(i, i ^ mask) for i in range(size)])


def kernel(rows, units, first, branch, tab, *refs):
    slots, refs = (None, refs) if first else (refs[0], refs[1:])
    own, a_hbm, refs = refs[0], refs[1], refs[2:]
    parts, refs = refs[: len(units)], refs[len(units) :]
    if first:
        out, slots_out, a_all, b_all, lefts, rights, sems, slots, sem = refs
    else:
        out, a_all, b_all, lefts, rights, sems = refs
    copies = [pltpu.make_async_copy(a_hbm, a_all, sems.at[0])]
    at = 0
    for part, n in zip(parts, units):
        copies.append(
            pltpu.make_async_copy(
                part, b_all.at[pl.ds(at * rows, n * rows)], sems.at[len(copies)]
            )
        )
        at += n
    for copy in copies:
        copy.start()
    nothing = 32 * rows
    b_all[nothing : nothing + BS, :] = jnp.zeros((BS, BS), jnp.bfloat16)

    def listed():
        mine = [slots[tab[32], j] for j in range(4)]

        def scan(p, counts):
            la, more = tab[p], []
            for j in range(4):
                m = slots[la, j]
                lefts[j * LIST + counts[j]] = la * rows + j * BS
                rights[j * LIST + counts[j]] = p * rows + m * BS
                more.append(counts[j] + (slots[32 + p, m] == mine[j]).astype(jnp.int32))
            return tuple(more)

        counts = lax.fori_loop(0, 32, scan, (jnp.int32(0),) * 4)
        for j in range(4):
            for k in range(3):
                lefts[j * LIST + counts[j] + k] = 0
                rights[j * LIST + counts[j] + k] = nothing
        return counts

    if not first:
        counts = listed()
    for copy in copies:
        copy.wait()
    if first:
        for base, whole in ((0, a_all), (32, b_all)):
            for k in range(32):
                row = whole[k * rows + ROWS : (k + 1) * rows, :].astype(jnp.float32)[0:1]
                slots_out[base + k : base + k + 1, :] = row.astype(jnp.int32)
        copy = pltpu.make_async_copy(slots_out, slots, sem)
        copy.start()
        copy.wait()
        counts = listed()

    for j in range(4):

        def four(t, total):
            at = [j * LIST + 4 * t + k for k in range(4)]
            left = [a_all[pl.ds(pl.multiple_of(lefts[i], 16), BS), :] for i in at]
            right = [b_all[pl.ds(pl.multiple_of(rights[i], 16), BS), :] for i in at]
            return total + jnp.dot(
                jnp.concatenate(left, 1),
                jnp.concatenate(right, 0),
                preferred_element_type=jnp.float32,
            )

        square = lax.fori_loop(0, (counts[j] + 3) // 4, four, jnp.zeros((BS, BS), jnp.float32))
        block = pl.ds(j * BS, BS)
        twice = 2.0 * own[block, :].astype(jnp.float32) - square
        out[block, :] = jnp.where(branch[0] == 1, twice, square).astype(out.dtype)


def multiply(branch, tab, slots, own, a_all, placed):
    first, rows = slots is None, own.shape[0]
    parts = [part for part, _ in placed]
    units = [len(names) for _, names in placed]
    smem = pl.BlockSpec(memory_space=pltpu.SMEM)
    vmem = pl.BlockSpec(memory_space=pltpu.VMEM)
    anywhere = pl.BlockSpec(memory_space=pl.ANY)
    out_shape = [jax.ShapeDtypeStruct((ROWS, BS), jnp.bfloat16)]
    scratch = [
        pltpu.VMEM((32 * rows, BS), jnp.bfloat16),
        pltpu.VMEM((32 * rows + BS, BS), jnp.bfloat16),
        pltpu.SMEM((4 * LIST,), jnp.int32),
        pltpu.SMEM((4 * LIST,), jnp.int32),
        pltpu.SemaphoreType.DMA((1 + len(parts),)),
    ]
    if first:
        out_shape.append(jax.ShapeDtypeStruct((64, BS), jnp.int32))
        scratch += [pltpu.SMEM((64, BS), jnp.int32), pltpu.SemaphoreType.DMA]
    done = pl.pallas_call(
        functools.partial(kernel, rows, units, first),
        out_shape=out_shape,
        in_specs=[smem] * (2 if first else 3) + [vmem] + [anywhere] * (1 + len(parts)),
        out_specs=[vmem] * len(out_shape),
        scratch_shapes=scratch,
        compiler_params=pltpu.CompilerParams(vmem_limit_bytes=52 * 1024 * 1024),
        cost_estimate=pl.CostEstimate(
            flops=2 * 128 * BS**3, bytes_accessed=64 * ROWS * BS * 2, transcendentals=0
        ),
    )(branch, tab, *([] if first else [slots]), own, a_all, *parts)
    return done[0], done[1] if first else slots


def gather(unit, pal, sibling, up, down):
    rows = unit.shape[0]
    near = jnp.concatenate([unit, pal])
    near, up, down = lax.optimization_barrier((near, up, down))
    a_all = lax.all_gather(near, ("x", "y"), axis=0, tiled=True)
    chains, first, second, sibling = ring(up, down, sibling)
    last = move(chains[0][6], hop)
    final = across(jnp.concatenate([chains[0][6], chains[1][6], last]), "core", 1)
    placed = [(unit, {0: (0, 0)}), (sibling, {0: (0, 1)})]
    for k in range(7):
        placed += [(chain[k], {0: (k + 1, w)}) for w, chain in enumerate(chains)]
    for part, start in ((first, 1), (second, 4)):
        placed.append((part, {i: (-(i // 2 + start), 1 - i % 2) for i in range(6)}))
    placed += [(last, {0: (8, 0)}), (final, {0: (-7, 1), 1: (-7, 0), 2: (8, 1)})]
    return a_all, placed


def ring(up, down, sibling):
    chains = [[up], [down]]

    def on():
        for chain in chains:
            chain.append(move(chain[-1], hop))

    def to_other(a, b):
        return across(jnp.concatenate([chain[k] for k in range(a, b) for chain in chains]), "core", 1)

    for _ in range(4):
        on()
    first = to_other(0, 3)
    on()
    chains[0][5], chains[1][5], first, sibling = lax.optimization_barrier(
        (chains[0][5], chains[1][5], first, sibling)
    )
    on()
    second = to_other(3, 6)
    chains[0][6], chains[1][6], second = lax.optimization_barrier((chains[0][6], chains[1][6], second))
    return chains, first, second, sibling


def table(placed):
    zh, zl, x, y, core = (lax.axis_index(name) for name in AXES)
    names = np.concatenate([np.array(list(n.values())) for _, n in placed])
    p = (zh - (1 - 2 * core) * names[:, 0]) % 16 * 2 + (core ^ names[:, 1])
    la = p // 2 * 2 + (p % 2 ^ zl)
    return jnp.concatenate([la, jnp.reshape((x * 4 + y) * 2, (1,))]).astype(jnp.int32)


def body(values, column_slot_index, branches):
    flat = values.reshape(ROWS, BS)
    tail = column_slot_index[:, 0].astype(jnp.bfloat16)[None]
    start = jnp.concatenate([flat, jnp.pad(tail, ((0, TAIL - 1), (0, BS - 4)))])
    def firsts(part, *steps):
        return [move(part, *steps, *more) for more in ((pair,), (flip,), (hop,), (flip, hop))]

    unit, others = move(start, swap), firsts(start, swap)
    slots = None
    for step in range(STEPS):
        if step:
            others = firsts(unit)
        a_all, placed = gather(unit, *others)
        unit, slots = multiply(
            branches[step : step + 1], table(placed), slots, unit, a_all, placed
        )
    return move(unit, swap).reshape(values.shape)


def solution(mesh):
    fine = Mesh(mesh.devices.reshape(SIZES), AXES)
    split = (("zh", "zl"), ("x", "y", "core"))
    in_specs = (P(*split, None, None), P(*split), P())
    return jax.shard_map(
        body, mesh=fine, in_specs=in_specs, out_specs=P(*split, None, None), check_vma=False
    )
```

```python
import functools

import jax
import jax.numpy as jnp
import numpy as np
from jax import lax
from jax.experimental import pallas as pl
from jax.experimental.pallas import tpu as pltpu
from jax.sharding import Mesh, PartitionSpec as P

STEPS = 2
BS = 128
ROWS = 4 * BS
LIST = 40
TAIL = 16
AXES = ("zh", "zl", "x", "y", "core")
SIZES = (16, 2, 4, 4, 2)


def swap(zh, zl, x, y, core):
    return zh, core, x, y, zl


def hop(zh, zl, x, y, core):
    return (zh + 1 - 2 * core) % 16, zl, x, y, core


def pair(zh, zl, x, y, core):
    return zh, 1 - zl, x, y, core


def flip(zh, zl, x, y, core):
    return zh, zl, x, y, 1 - core


def move(part, *steps):
    pairs = []
    for i in range(1024):
        place = tuple(int(k) for k in np.unravel_index(i, SIZES))
        for step in steps:
            place = step(*place)
        pairs.append((i, int(np.ravel_multi_index(place, SIZES))))
    return lax.ppermute(part, AXES, pairs)


def across(part, axis, mask):
    size = SIZES[AXES.index(axis)]
    return lax.ppermute(part, axis, [(i, i ^ mask) for i in range(size)])


def kernel(rows, units, first, branch, tab, *refs):
    slots, refs = (None, refs) if first else (refs[0], refs[1:])
    own, a_hbm, refs = refs[0], refs[1], refs[2:]
    parts, refs = refs[: len(units)], refs[len(units) :]
    if first:
        out, slots_out, a_all, b_all, lefts, rights, sems, slots, sem = refs
    else:
        out, a_all, b_all, lefts, rights, sems = refs
    copies = [pltpu.make_async_copy(a_hbm, a_all, sems.at[0])]
    at = 0
    for part, n in zip(parts, units):
        copies.append(
            pltpu.make_async_copy(
                part, b_all.at[pl.ds(at * rows, n * rows)], sems.at[len(copies)]
            )
        )
        at += n
    for copy in copies:
        copy.start()
    nothing = 32 * rows
    b_all[nothing : nothing + BS, :] = jnp.zeros((BS, BS), jnp.bfloat16)

    def listed():
        mine = [slots[tab[32], j] for j in range(4)]

        def scan(p, counts):
            la, more = tab[p], []
            for j in range(4):
                m = slots[la, j]
                lefts[j * LIST + counts[j]] = la * rows + j * BS
                rights[j * LIST + counts[j]] = p * rows + m * BS
                more.append(counts[j] + (slots[32 + p, m] == mine[j]).astype(jnp.int32))
            return tuple(more)

        counts = lax.fori_loop(0, 32, scan, (jnp.int32(0),) * 4)
        for j in range(4):
            for k in range(3):
                lefts[j * LIST + counts[j] + k] = 0
                rights[j * LIST + counts[j] + k] = nothing
        return counts

    if not first:
        counts = listed()
    for copy in copies:
        copy.wait()
    if first:
        for base, whole in ((0, a_all), (32, b_all)):
            for k in range(32):
                row = whole[k * rows + ROWS : (k + 1) * rows, :].astype(jnp.float32)[0:1]
                slots_out[base + k : base + k + 1, :] = row.astype(jnp.int32)
        copy = pltpu.make_async_copy(slots_out, slots, sem)
        copy.start()
        copy.wait()
        counts = listed()

    for j in range(4):

        def four(t, total):
            at = [j * LIST + 4 * t + k for k in range(4)]
            left = [a_all[pl.ds(pl.multiple_of(lefts[i], 16), BS), :] for i in at]
            right = [b_all[pl.ds(pl.multiple_of(rights[i], 16), BS), :] for i in at]
            return total + jnp.dot(
                jnp.concatenate(left, 1),
                jnp.concatenate(right, 0),
                preferred_element_type=jnp.float32,
            )

        square = lax.fori_loop(0, (counts[j] + 3) // 4, four, jnp.zeros((BS, BS), jnp.float32))
        block = pl.ds(j * BS, BS)
        twice = 2.0 * own[block, :].astype(jnp.float32) - square
        out[block, :] = jnp.where(branch[0] == 1, twice, square).astype(out.dtype)


def multiply(branch, tab, slots, own, a_all, placed):
    first, rows = slots is None, own.shape[0]
    parts = [part for part, _ in placed]
    units = [len(names) for _, names in placed]
    smem = pl.BlockSpec(memory_space=pltpu.SMEM)
    vmem = pl.BlockSpec(memory_space=pltpu.VMEM)
    anywhere = pl.BlockSpec(memory_space=pl.ANY)
    out_shape = [jax.ShapeDtypeStruct((ROWS, BS), jnp.bfloat16)]
    scratch = [
        pltpu.VMEM((32 * rows, BS), jnp.bfloat16),
        pltpu.VMEM((32 * rows + BS, BS), jnp.bfloat16),
        pltpu.SMEM((4 * LIST,), jnp.int32),
        pltpu.SMEM((4 * LIST,), jnp.int32),
        pltpu.SemaphoreType.DMA((1 + len(parts),)),
    ]
    if first:
        out_shape.append(jax.ShapeDtypeStruct((64, BS), jnp.int32))
        scratch += [pltpu.SMEM((64, BS), jnp.int32), pltpu.SemaphoreType.DMA]
    done = pl.pallas_call(
        functools.partial(kernel, rows, units, first),
        out_shape=out_shape,
        in_specs=[smem] * (2 if first else 3) + [vmem] + [anywhere] * (1 + len(parts)),
        out_specs=[vmem] * len(out_shape),
        scratch_shapes=scratch,
        compiler_params=pltpu.CompilerParams(vmem_limit_bytes=52 * 1024 * 1024),
        cost_estimate=pl.CostEstimate(
            flops=2 * 128 * BS**3, bytes_accessed=64 * ROWS * BS * 2, transcendentals=0
        ),
    )(branch, tab, *([] if first else [slots]), own, a_all, *parts)
    return done[0], done[1] if first else slots


def gather(unit, pal, sibling, up, down):
    rows = unit.shape[0]
    near = jnp.concatenate([unit, pal])
    near, up, down = lax.optimization_barrier((near, up, down))
    a_all = lax.all_gather(near, ("x", "y"), axis=0, tiled=True)
    chains, first, second, sibling = ring(up, down, sibling)
    last = move(chains[0][6], hop)
    seven = across(jnp.concatenate([chains[0][6], chains[1][6]]), "core", 1)
    last, seven = lax.optimization_barrier((last, seven))
    eight = across(last, "core", 1)
    placed = [(unit, {0: (0, 0)}), (sibling, {0: (0, 1)})]
    for k in range(7):
        placed += [(chain[k], {0: (k + 1, w)}) for w, chain in enumerate(chains)]
    for part, start in ((first, 1), (second, 4)):
        placed.append((part, {i: (-(i // 2 + start), 1 - i % 2) for i in range(6)}))
    placed += [(last, {0: (8, 0)}), (seven, {0: (-7, 1), 1: (-7, 0)}), (eight, {0: (8, 1)})]
    return a_all, placed


def ring(up, down, sibling):
    chains = [[up], [down]]

    def on():
        for chain in chains:
            chain.append(move(chain[-1], hop))

    def to_other(a, b):
        return across(jnp.concatenate([chain[k] for k in range(a, b) for chain in chains]), "core", 1)

    for _ in range(4):
        on()
    first = to_other(0, 3)
    on()
    chains[0][5], chains[1][5], first, sibling = lax.optimization_barrier(
        (chains[0][5], chains[1][5], first, sibling)
    )
    on()
    second = to_other(3, 6)
    chains[0][6], chains[1][6], second = lax.optimization_barrier((chains[0][6], chains[1][6], second))
    return chains, first, second, sibling


def table(placed):
    zh, zl, x, y, core = (lax.axis_index(name) for name in AXES)
    names = np.concatenate([np.array(list(n.values())) for _, n in placed])
    p = (zh - (1 - 2 * core) * names[:, 0]) % 16 * 2 + (core ^ names[:, 1])
    la = p // 2 * 2 + (p % 2 ^ zl)
    return jnp.concatenate([la, jnp.reshape((x * 4 + y) * 2, (1,))]).astype(jnp.int32)


def body(values, column_slot_index, branches):
    flat = values.reshape(ROWS, BS)
    tail = column_slot_index[:, 0].astype(jnp.bfloat16)[None]
    start = jnp.concatenate([flat, jnp.pad(tail, ((0, TAIL - 1), (0, BS - 4)))])
    def firsts(part, *steps):
        return [move(part, *steps, *more) for more in ((pair,), (flip,), (hop,), (flip, hop))]

    unit, others = move(start, swap), firsts(start, swap)
    slots = None
    for step in range(STEPS):
        if step:
            others = firsts(unit)
        a_all, placed = gather(unit, *others)
        unit, slots = multiply(
            branches[step : step + 1], table(placed), slots, unit, a_all, placed
        )
    return move(unit, swap).reshape(values.shape)


def solution(mesh):
    fine = Mesh(mesh.devices.reshape(SIZES), AXES)
    split = (("zh", "zl"), ("x", "y", "core"))
    in_specs = (P(*split, None, None), P(*split), P())
    return jax.shard_map(
        body, mesh=fine, in_specs=in_specs, out_specs=P(*split, None, None), check_vma=False
    )
```
